256 devices in a mesh: blk: 16 (over z, y_lo), rows: 16 (over x, y_hi, core).
Axes of the slice: x: 4, y: 4 (y_hi: 2, y_lo: 2; y = y_hi * 2 + y_lo), z: 8, core: 2. Of those that a mesh axis runs over, the one named last changes fastest.
Arguments:
- a_tiles: bfloat16 [262144, 1024], P(('blk', 'rows')), may hold values from -0.1875 to 0.1875
- a_cols: int32 [4096, 16], P(('blk', 'rows')), may hold values from 0 to 255
- p_tiles: bfloat16 [262144, 128], P(('blk', 'rows')), may hold values from -3 to 3
- p_cols: int32 [4096, 2], P(('blk', 'rows')), may hold values from 0 to 1
- band_shift: int32 [1], replicated, may hold values from 1 to 15
Outputs:
- coarse: bfloat16 [32768, 2, 2048], P(('blk', 'rows'))
The draws below stay inside these ranges and needn't reach their ends.
Inputs may be any that keep to these rules, and one draw needn't show every extreme that they name: `a_cols`: the entries are positions in a row group of 256 fine block rows: the first 12 of a block row in its own group, the last 4 in the group band_shift further around the loop. `p_cols`: each entry picks one of the 2 coarse blocks of the device that holds the fine block row.
All inputs are finite; a program needn't handle non-finite values.
Results may differ from the reference program's by a relative error of at most 0.005.
Values may be sent and summed in bfloat16 or wider, within the bound.
No kernel may reach another device: no remote copies, remote signals or barrier semaphores. Data moves between devices by JAX's collectives and lax.ppermute only.
A program may use at most 128 MiB of HBM per device.

```python
import jax
import jax.numpy as jnp
from jax import lax

B = 64
FB_DEV = 16
KL = 12
KP = 2
KA = 16
CB_DEV = 2
GROUP = 256
GC = 32
FB = 4096
CB = 512
N_BLK = 16
N_ROWS = 16


def set_ends(array, key, smallest, high):
    longest = array.shape.index(max(array.shape))
    spots = []
    for shift in (0, 1):
        where = [jax.random.randint(jax.random.fold_in(key, axis), (), 0, length) for axis, length in enumerate(array.shape)]
        where[longest] = (where[longest] + shift) % array.shape[longest]
        spots.append(tuple(where))
    return array.at[spots[0]].set(smallest).at[spots[1]].set(high)


def block_levels(rng, extent, cuts, smallest, high):
    def one(position, blocks):
        heights = jax.random.uniform(jax.random.fold_in(jax.random.fold_in(rng, 6), position), (blocks,), jnp.float32, smallest / len(cuts), high / len(cuts))
        return jnp.repeat(jnp.exp(heights), extent[position] // blocks).reshape((-1,) + (1,) * (len(extent) - position - 1))

    loudness = one(*cuts[0])
    for cut in cuts[1:]:
        loudness = loudness * one(*cut)
    return loudness


def scatter_about(stream_key, dims, scale, bound, shards=(), held_as=jnp.bfloat16):
    drawn = scale * jax.random.normal(stream_key, dims, jnp.float32)
    if shards:
        drawn = drawn * block_levels(stream_key, dims, shards, -0.22, 0.18)
    return jnp.clip(drawn, -bound, bound).astype(held_as)


def setup_inputs(seed: int = 0) -> dict:
    streams_of = jax.random.split(jax.random.key(seed), 6)
    a_tiles = scatter_about(streams_of[0], (FB * B, KA * B), (KA * B) ** -0.5, 0.1875, ((0, 256),))
    a_cols = set_ends(jax.random.randint(streams_of[1], (FB, KA), 0, GROUP), jax.random.fold_in(streams_of[1], 1), 0, GROUP - 1).astype(jnp.int32)
    p_tiles = scatter_about(streams_of[2], (FB * B, KP * B), 0.5, 3.0, ((0, 256),))
    p_cols = set_ends(jax.random.randint(streams_of[3], (FB, KP), 0, CB_DEV), jax.random.fold_in(streams_of[3], 1), 0, CB_DEV - 1).astype(jnp.int32)
    band_shift = jax.random.randint(streams_of[4], (1,), 1, N_BLK).astype(jnp.int32)
    return {"a_tiles": a_tiles, "a_cols": a_cols, "p_tiles": p_tiles, "p_cols": p_cols, "band_shift": band_shift}


def slot_terms(a_half, col_half, panel_four, panel_cols, own_four, own_cols):
    row_count, kcount = col_half.shape
    slots = kcount * KP
    flat_cols = col_half.reshape(-1).astype(jnp.int32)
    picked = jnp.take(panel_four, flat_cols, axis=0).reshape(row_count, kcount, B, KP, B)
    products = jnp.einsum("irkq,ikqnc->iknrc", a_half.astype(jnp.float32), picked.astype(jnp.float32), precision=lax.Precision.HIGHEST)
    products = products.reshape(row_count, slots, B, B).astype(jnp.bfloat16)
    coarse_col = jnp.take(panel_cols, flat_cols, axis=0).reshape(row_count, kcount, KP)
    coarse_col = (coarse_col + (col_half // FB_DEV)[:, :, None] * CB_DEV).reshape(row_count, slots).astype(jnp.int32)
    contrib = jnp.einsum("irmq,isrc->imsqc", own_four.astype(jnp.float32), products.astype(jnp.float32), precision=lax.Precision.HIGHEST)
    seg_keys = (own_cols[:, :, None] * GC + coarse_col[:, None, :]).astype(jnp.int32)
    return jax.ops.segment_sum(contrib.reshape(-1, B * B), seg_keys.reshape(-1), num_segments=CB_DEV * GC)


def reference(a_tiles, a_cols, p_tiles, p_cols, band_shift):
    devices = N_BLK * N_ROWS
    a_four = a_tiles.reshape(devices, FB_DEV, B, KA, B)
    a_split = a_cols.reshape(devices, FB_DEV, KA)
    panels = p_tiles.reshape(N_BLK, GROUP, B, KP, B)
    panel_cols = p_cols.reshape(N_BLK, GROUP, KP)
    own_four = p_tiles.reshape(devices, FB_DEV, B, KP, B)
    own_cols = p_cols.reshape(devices, FB_DEV, KP)

    def per_device(device):
        group_idx = device // N_ROWS
        band_group = (group_idx + band_shift[0]) % N_BLK
        tiles_here = a_four[device]
        cols_here = a_split[device]
        local_half = slot_terms(tiles_here[:, :, :KL], cols_here[:, :KL], panels[group_idx], panel_cols[group_idx], own_four[device], own_cols[device])
        band_half = slot_terms(tiles_here[:, :, KL:], cols_here[:, KL:], panels[band_group], panel_cols[band_group], own_four[device], own_cols[device])
        halves = jnp.stack([local_half, band_half], axis=1).reshape(CB_DEV, GC, 2, B, B)
        return halves.transpose(0, 3, 2, 1, 4).reshape(CB_DEV * B, 2, GC * B).astype(jnp.bfloat16)

    result = lax.map(per_device, jnp.arange(devices, dtype=jnp.int32))
    return result.reshape(CB * B, 2, GC * B)
```

```python
import functools

import jax
import jax.numpy as jnp
from jax import lax
from jax.experimental import pallas as pl
from jax.experimental.pallas import tpu as pltpu
from jax.sharding import PartitionSpec as P

B = 64
KL = 12
F32 = jnp.float32
BF16 = jnp.bfloat16
LIMIT = 40 * 1024 * 1024


def rows_id(x, y, c):
    return (x * 2 + y) * 2 + c


def rows_pairs(move):
    return [
        (rows_id(x, y, c), rows_id(*move(x, y, c)))
        for x in range(4)
        for y in range(2)
        for c in range(2)
    ]


CORE_SWAP = rows_pairs(lambda x, y, c: (x, y, 1 - c))
Y_SWAP = rows_pairs(lambda x, y, c: (x, 1 - y, c))
X_UP = rows_pairs(lambda x, y, c: ((x + 1) % 4, y, c))
X_DOWN = rows_pairs(lambda x, y, c: ((x + 3) % 4, y, c))


def lift_kernel(cols_ref, p_ref, g_ref):
    lane = lax.broadcasted_iota(jnp.int32, (B, 2 * B), 1)
    low = lane < B
    for i in range(p_ref.shape[0] // B):
        here = pl.ds(i * B, B)
        first = cols_ref[i, 0].astype(F32)
        second = cols_ref[i, 1].astype(F32)
        straight = p_ref[here, :].astype(F32)
        crossed = pltpu.roll(straight, B, 1)
        keep = jnp.where(low, 1.0 - first, second)
        cross = jnp.where(low, 1.0 - second, first)
        g_ref[here, :] = (straight * keep + crossed * cross).astype(BF16)


def lift(p_tiles, p_cols):
    return pl.pallas_call(
        lift_kernel,
        out_shape=jax.ShapeDtypeStruct(p_tiles.shape, BF16),
        in_specs=[
            pl.BlockSpec(memory_space=pltpu.SMEM),
            pl.BlockSpec(memory_space=pltpu.VMEM),
        ],
        out_specs=pl.BlockSpec(memory_space=pltpu.VMEM),
    )(p_cols, p_tiles)


def left_kernel(g_ref, a_ref, w_ref):
    g_t = g_ref[...].T
    w_ref[0] = jnp.dot(g_t, a_ref[...], preferred_element_type=F32).astype(BF16)


def left(lifted, a_tiles):
    rows = a_tiles.shape[0] // B
    width = a_tiles.shape[1]
    return pl.pallas_call(
        left_kernel,
        grid=(rows,),
        out_shape=jax.ShapeDtypeStruct((rows, 2 * B, width), BF16),
        in_specs=[
            pl.BlockSpec((B, 2 * B), lambda i: (i, 0)),
            pl.BlockSpec((B, width), lambda i: (i, 0)),
        ],
        out_specs=pl.BlockSpec((1, 2 * B, width), lambda i: (i, 0, 0)),
    )(lifted, a_tiles)


def half_kernel(k_from, k_to, sizes, row_ref, dev_ref, *refs):
    pieces = refs[: len(sizes)]
    w_ref, out_ref, panel, acc, sems = refs[len(sizes) :]
    copies = []
    start = 0
    for n, (piece, size) in enumerate(zip(pieces, sizes)):
        copy = pltpu.make_async_copy(piece, panel.at[pl.ds(start, size), :], sems.at[n])
        copy.start()
        copies.append(copy)
        start += size
    acc[...] = jnp.zeros_like(acc)
    for copy in copies:
        copy.wait()
    blank = jnp.zeros((B, 2 * B), BF16)

    def step(i, carry):
        for k in range(k_from, k_to, 2):
            upper = panel[pl.ds(pl.multiple_of(row_ref[i, k] * B, B), B), :]
            lower = panel[pl.ds(pl.multiple_of(row_ref[i, k + 1] * B, B), B), :]
            right = jnp.concatenate(
                [
                    jnp.concatenate([upper, blank], axis=1),
                    jnp.concatenate([blank, lower], axis=1),
                ],
                axis=0,
            )
            both = jnp.dot(
                w_ref[i, :, k * B : (k + 2) * B], right, preferred_element_type=F32
            )
            acc[dev_ref[i, k]] += both[:, : 2 * B]
            acc[dev_ref[i, k + 1]] += both[:, 2 * B :]
        return carry

    lax.fori_loop(0, w_ref.shape[0], step, 0)
    for d in range(acc.shape[0]):
        out_ref[:, d * 2 * B : (d + 1) * 2 * B] = acc[d].astype(BF16)


def half(k_from, k_to, row_of, dev_of, pieces, w):
    sizes = tuple(piece.shape[0] for piece in pieces)
    devs = sum(sizes) // (16 * B)
    return pl.pallas_call(
        functools.partial(half_kernel, k_from, k_to, sizes),
        out_shape=jax.ShapeDtypeStruct((2 * B, devs * 2 * B), BF16),
        in_specs=[pl.BlockSpec(memory_space=pltpu.SMEM)] * 2
        + [pl.BlockSpec(memory_space=pl.ANY)] * len(pieces)
        + [pl.BlockSpec(memory_space=pltpu.VMEM)],
        out_specs=pl.BlockSpec(memory_space=pltpu.VMEM),
        scratch_shapes=[
            pltpu.VMEM((sum(sizes), 2 * B), BF16),
            pltpu.VMEM((devs, 2 * B, 2 * B), F32),
            pltpu.SemaphoreType.DMA((len(sizes),)),
        ],
        compiler_params=pltpu.CompilerParams(vmem_limit_bytes=LIMIT),
    )(row_of, dev_of, *pieces, w)


def gather_panel(own):
    rows = own.shape[0]
    beside = lax.ppermute(own, "rows", Y_SWAP)
    base = jnp.concatenate([own, beside], axis=0)
    from_left = lax.ppermute(base, "rows", X_UP)
    from_right = lax.ppermute(base, "rows", X_DOWN)
    far_first = lax.ppermute(from_left[:rows], "rows", X_UP)
    far_second = lax.ppermute(from_right[rows:], "rows", X_DOWN)
    same = [base, from_left, from_right, far_first, far_second]
    other = [lax.ppermute(piece, "rows", CORE_SWAP) for piece in same]
    return same + other


def slot_of(dev):
    me = lax.axis_index("rows")
    x, y, c = me // 4, me // 2 % 2, me % 2
    dx, dy, dc = (dev // 4 - x) % 4, (dev // 2 + y) % 2, (dev + c) % 2
    place = jnp.where(dx == 0, 0, jnp.where(dx == 3, 1, jnp.where(dx == 1, 2, 3)))
    return (dc * 4 + place) * 2 + dy


def per_device(a_tiles, a_cols, p_tiles, p_cols, band_shift):
    fb_dev = a_cols.shape[0]
    count = lax.axis_size("blk")
    own = lift(p_tiles, p_cols)
    dev_of = a_cols // fb_dev
    row_of = slot_of(dev_of) * fb_dev + a_cols % fb_dev

    def shifted(steps):
        return lambda value: lax.ppermute(
            value, "blk", [(s, (s - steps) % count) for s in range(count)]
        )

    band = lax.switch(band_shift[0] - 1, [shifted(n) for n in range(1, count)], own)
    near_pieces = gather_panel(own)
    far_pieces = gather_panel(band)
    w = left(own, a_tiles)
    near = half(0, KL, row_of, dev_of, near_pieces, w)
    far = half(KL, a_cols.shape[1], row_of, dev_of, far_pieces, w)
    return jnp.stack([near, far], axis=1)


def solution(mesh):
    return jax.shard_map(
        per_device,
        mesh=mesh,
        in_specs=(
            P(("blk", "rows"), None),
            P(("blk", "rows"), None),
            P(("blk", "rows"), None),
            P(("blk", "rows"), None),
            P(),
        ),
        out_specs=P(("blk", "rows"), None, None),
        check_vma=False,
    )
```

```python
import functools

import jax
import jax.numpy as jnp
from jax import lax
from jax.experimental import pallas as pl
from jax.experimental.pallas import tpu as pltpu
from jax.sharding import PartitionSpec as P

B = 64
KL = 12
F32 = jnp.float32
BF16 = jnp.bfloat16
ALL = 60 * 1024 * 1024
LIMIT = 16 * 1024 * 1024
SCALARS = pl.BlockSpec(memory_space=pltpu.SMEM)
VECTORS = pl.BlockSpec(memory_space=pltpu.VMEM)


def cost(micros):
    return pl.CostEstimate(flops=0, bytes_accessed=int(micros * 3.5e6), transcendentals=0)


def rows_id(x, y, c):
    return (x * 2 + y) * 2 + c


def rows_pairs(move):
    return [
        (rows_id(x, y, c), rows_id(*move(x, y, c)))
        for x in range(4)
        for y in range(2)
        for c in range(2)
    ]


X_UP, X_DOWN, Y_OVER, BOTH = (1, 0), (3, 0), (0, 1), (1, 1)
STEPS = (
    (0, X_UP, X_UP),
    (0, X_DOWN, X_DOWN),
    (0, Y_OVER, Y_OVER),
    (1, X_UP, Y_OVER),
    (2, Y_OVER, X_DOWN),
    (3, X_UP, X_DOWN),
    (4, Y_OVER, X_UP),
)
CORE_SWAP = rows_pairs(lambda x, y, c: (x, y, 1 - c))
STEP_PAIRS = tuple(
    rows_pairs(
        lambda x, y, c, step=step: ((x + step[1 + c][0]) % 4, (y + step[1 + c][1]) % 2, c)
    )
    for step in STEPS
)


def origins():
    held = [[(0, 0)], [(0, 0)]]
    for source, *moves in STEPS:
        for c in (0, 1):
            x, y = held[c][source]
            held[c].append(((x - moves[c][0]) % 4, (y - moves[c][1]) % 2))
    return held


def lift_kernel(me_ref, cols_ref, p_ref, a_cols_ref, g_ref, row_ref, dev_ref):
    lane = lax.broadcasted_iota(jnp.int32, (B, 2 * B), 1)
    low = lane < B

    def step(i, carry):
        here = pl.ds(pl.multiple_of(i * B, B), B)
        first = cols_ref[0, i].astype(F32)
        second = cols_ref[1, i].astype(F32)
        straight = p_ref[here, :].astype(F32)
        crossed = pltpu.roll(straight, B, 1)
        keep = jnp.where(low, 1.0 - first, second)
        cross = jnp.where(low, 1.0 - second, first)
        g_ref[here, :] = (straight * keep + crossed * cross).astype(BF16)
        return carry

    lax.fori_loop(0, p_ref.shape[0] // B, step, 0, unroll=4)
    me = me_ref[0]
    x, y, c = me >> 2, (me >> 1) & 1, me & 1
    j = a_cols_ref[...]
    dev = j >> 4
    key = ((dev & 1) * 4 + (((dev >> 2) - x) & 3)) * 2 + (((dev >> 1) - y) & 1)
    place = jnp.zeros_like(dev)
    for core, held in enumerate(origins()):
        for n, (dx, dy) in enumerate(held):
            place = jnp.where(key == (core * 4 + dx) * 2 + dy, n, place)
    slot = ((dev - c) & 1) * 8 + place
    row_ref[...] = slot * 16 + (j & 15)
    dev_ref[...] = dev


def lift(p_tiles, p_cols, a_cols):
    table = jax.ShapeDtypeStruct(a_cols.shape, jnp.int32)
    return pl.pallas_call(
        lift_kernel,
        out_shape=(jax.ShapeDtypeStruct(p_tiles.shape, BF16), table, table),
        in_specs=[SCALARS, SCALARS, VECTORS, VECTORS],
        out_specs=(VECTORS, VECTORS, VECTORS),
        compiler_params=pltpu.CompilerParams(vmem_limit_bytes=ALL),
    )(lax.axis_index("rows").astype(jnp.int32)[None], p_cols.T, p_tiles, a_cols)


def left_kernel(g_ref, a_ref, w_ref):
    def step(n, carry):
        here = pl.ds(pl.multiple_of(n * 2 * B, 2 * B), 2 * B)
        g_t = g_ref[here, :].T
        a_two = a_ref[here, :]
        for m in (0, 1):
            w_ref[2 * n + m] = jnp.dot(
                g_t[:, m * B : (m + 1) * B],
                a_two[m * B : (m + 1) * B, :],
                preferred_element_type=F32,
            ).astype(BF16)
        return carry

    lax.fori_loop(0, w_ref.shape[0] // 2, step, 0, unroll=2)


def left(lifted, a_tiles):
    rows = a_tiles.shape[0] // B
    width = a_tiles.shape[1]
    return pl.pallas_call(
        left_kernel,
        out_shape=jax.ShapeDtypeStruct((rows, 2 * B, width), BF16),
        in_specs=[VECTORS, VECTORS],
        out_specs=VECTORS,
        cost_estimate=cost(3.0),
        compiler_params=pltpu.CompilerParams(vmem_limit_bytes=LIMIT),
    )(lifted, a_tiles)


def add_products(k_from, k_to, unroll, row_ref, dev_ref, pieces, w_ref, panel, acc, sems):
    copies = []
    start = 0
    for n, piece in enumerate(pieces):
        size = piece.shape[0]
        copies.append(
            pltpu.make_async_copy(piece, panel.at[pl.ds(start, size), :], sems.at[n])
        )
        copies[-1].start()
        start += size
    acc[...] = jnp.zeros_like(acc)
    for copy in copies:
        copy.wait()
    blank = jnp.zeros((B, 2 * B), BF16)

    def step(i, carry):
        for k in range(k_from, k_to, 2):
            upper = panel[pl.ds(pl.multiple_of(row_ref[i, k] * B, B), B), :]
            lower = panel[pl.ds(pl.multiple_of(row_ref[i, k + 1] * B, B), B), :]
            right = jnp.concatenate(
                [
                    jnp.concatenate([upper, blank], axis=1),
                    jnp.concatenate([blank, lower], axis=1),
                ],
                axis=0,
            )
            both = jnp.dot(
                w_ref[i, :, k * B : (k + 2) * B], right, preferred_element_type=F32
            )
            acc[dev_ref[i, k]] += both[:, : 2 * B]
            acc[dev_ref[i, k + 1]] += both[:, 2 * B :]
        return carry

    lax.fori_loop(0, w_ref.shape[0], step, 0, unroll=unroll)


def near_kernel(count, row_ref, dev_ref, *refs):
    w_ref, out_ref, panel, acc, sems = refs[count:]
    add_products(0, KL, 2, row_ref, dev_ref, refs[:count], w_ref, panel, acc, sems)

    def finish(d, carry):
        out_ref[d] = acc[d].astype(BF16)
        return carry

    lax.fori_loop(0, acc.shape[0], finish, 0, unroll=2)


def far_kernel(count, row_ref, dev_ref, *refs):
    w_ref, near_ref, out_ref, panel, acc, sems, mixed = refs[count:]
    ka = row_ref.shape[1]
    add_products(KL, ka, 4, row_ref, dev_ref, refs[:count], w_ref, panel, acc, sems)

    def finish(d, carry):
        lanes = pl.ds(pl.multiple_of(d * 2 * B, 2 * B), 2 * B)
        slot = d % 2
        mixed[slot, pl.ds(0, 2 * B, stride=2), :] = near_ref[d].astype(F32)
        mixed[slot, pl.ds(1, 2 * B, stride=2), :] = acc[d]
        out_ref[:, :, lanes] = mixed[slot].astype(BF16).reshape(2 * B, 2, 2 * B)
        return carry

    lax.fori_loop(0, acc.shape[0], finish, 0, unroll=2)


def products(kernel, row_of, dev_of, pieces, others, out_shape, more, micros):
    rows = sum(piece.shape[0] for piece in pieces)
    devs = rows // (16 * B)
    return pl.pallas_call(
        functools.partial(kernel, len(pieces)),
        out_shape=jax.ShapeDtypeStruct(out_shape, BF16),
        in_specs=[SCALARS] * 2 + [VECTORS] * (len(pieces) + len(others)),
        out_specs=VECTORS,
        scratch_shapes=[
            pltpu.VMEM((rows, 2 * B), BF16),
            pltpu.VMEM((devs, 2 * B, 2 * B), F32),
            pltpu.SemaphoreType.DMA((len(pieces),)),
            *more,
        ],
        cost_estimate=cost(micros),
        compiler_params=pltpu.CompilerParams(vmem_limit_bytes=LIMIT),
    )(row_of, dev_of, *pieces, *others)


def near_half(row_of, dev_of, pieces, w):
    devs = sum(piece.shape[0] for piece in pieces) // (16 * B)
    shape = (devs, 2 * B, 2 * B)
    return products(near_kernel, row_of, dev_of, pieces, (w,), shape, (), 5.0)


def far_half(row_of, dev_of, pieces, w, near):
    shape = (2 * B, 2, near.shape[0] * 2 * B)
    more = (pltpu.VMEM((2, 4 * B, 2 * B), F32),)
    return products(far_kernel, row_of, dev_of, pieces, (w, near), shape, more, 4.0)


def step(n, sent):
    return lax.ppermute(sent, "rows", STEP_PAIRS[n])


def swapped(piece):
    return lax.ppermute(piece, "rows", CORE_SWAP)


def early(own):
    return step(0, own), step(1, own), step(2, own)


def late(*held):
    held = [None, *held]
    for n in range(3, len(STEPS)):
        held.append(step(n, held[STEPS[n][0]]))
    return held[4:]


def per_device(a_tiles, a_cols, p_tiles, p_cols, band_shift):
    count = lax.axis_size("blk")
    own, row_of, dev_of = lift(p_tiles, p_cols, a_cols)

    always = band_shift[0] > 0

    def begin(own):
        first = early(own)
        return *first, *late(*first)

    def nothing(own):
        return (own,) * len(STEPS)

    def turned(steps):
        pairs = [(s, (s - steps) % count) for s in range(count)]

        def run(own):
            band = lax.ppermute(own, "blk", pairs)
            held = lax.cond(always, begin, nothing, own)
            return lax.optimization_barrier((band, *held))

        return run

    band, *near_held = lax.switch(
        band_shift[0] - 1, [turned(steps) for steps in range(1, count)], own
    )
    w = left(own, a_tiles)
    first = early(band)
    *first, w = lax.optimization_barrier((*first, w))
    far_held = [band, *first]
    near_held = [own, *near_held]
    near_pieces = near_held + [swapped(piece) for piece in near_held]
    near = near_half(row_of, dev_of, near_pieces, w)
    far_late = late(*far_held[1:])
    *far_late, near = lax.optimization_barrier((*far_late, near))
    far_held += far_late
    far_pieces = far_held + [swapped(piece) for piece in far_held]
    return far_half(row_of, dev_of, far_pieces, w, near)


def solution(mesh):
    return jax.shard_map(
        per_device,
        mesh=mesh,
        in_specs=(
            P(("blk", "rows"), None),
            P(("blk", "rows"), None),
            P(("blk", "rows"), None),
            P(("blk", "rows"), None),
            P(),
        ),
        out_specs=P(("blk", "rows"), None, None),
        check_vma=False,
    )
```

```python
import functools

import jax
import jax.numpy as jnp
from jax import lax
from jax.experimental import pallas as pl
from jax.experimental.pallas import tpu as pltpu
from jax.sharding import PartitionSpec as P

B = 64
KL = 12
F32 = jnp.float32
BF16 = jnp.bfloat16
ALL = 60 * 1024 * 1024
LIMIT = 16 * 1024 * 1024
SCALARS = pl.BlockSpec(memory_space=pltpu.SMEM)
VECTORS = pl.BlockSpec(memory_space=pltpu.VMEM)


def cost(micros):
    return pl.CostEstimate(flops=0, bytes_accessed=int(micros * 3.5e6), transcendentals=0)


def rows_id(x, y, c):
    return (x * 2 + y) * 2 + c


def rows_pairs(move):
    return [
        (rows_id(x, y, c), rows_id(*move(x, y, c)))
        for x in range(4)
        for y in range(2)
        for c in range(2)
    ]


X_UP, X_DOWN, Y_OVER, BOTH = (1, 0), (3, 0), (0, 1), (1, 1)
NEAR_STEPS = (
    (0, X_UP, X_UP),
    (0, X_DOWN, X_DOWN),
    (0, Y_OVER, Y_OVER),
    (0, BOTH, BOTH),
    (3, X_DOWN, X_DOWN),
    (1, X_UP, X_UP),
    (4, X_UP, X_UP),
)
FAR_STEPS = (
    (0, X_UP, X_UP),
    (0, X_DOWN, X_DOWN),
    (0, Y_OVER, Y_OVER),
    (1, X_UP, Y_OVER),
    (2, Y_OVER, X_DOWN),
    (3, X_UP, X_DOWN),
    (4, Y_OVER, X_UP),
)
CORE_SWAP = rows_pairs(lambda x, y, c: (x, y, 1 - c))


def moved(step, held):
    source, *moves = step
    pairs = rows_pairs(
        lambda x, y, c: ((x + moves[c][0]) % 4, (y + moves[c][1]) % 2, c)
    )
    return lax.ppermute(held[source], "rows", pairs)


def origins(steps):
    held = [[(0, 0)], [(0, 0)]]
    for source, *moves in steps:
        for c in (0, 1):
            x, y = held[c][source]
            held[c].append(((x - moves[c][0]) % 4, (y - moves[c][1]) % 2))
    return held


def places(key, steps):
    place = jnp.zeros_like(key)
    for core, held in enumerate(origins(steps)):
        for n, (dx, dy) in enumerate(held):
            place = jnp.where(key == (core * 4 + dx) * 2 + dy, n, place)
    return place


def lift_kernel(me_ref, cols_ref, p_ref, a_cols_ref, g_ref, row_ref, dev_ref):
    lane = lax.broadcasted_iota(jnp.int32, (B, 2 * B), 1)
    low = lane < B

    def step(i, carry):
        here = pl.ds(pl.multiple_of(i * B, B), B)
        first = cols_ref[0, i].astype(F32)
        second = cols_ref[1, i].astype(F32)
        straight = p_ref[here, :].astype(F32)
        crossed = pltpu.roll(straight, B, 1)
        keep = jnp.where(low, 1.0 - first, second)
        cross = jnp.where(low, 1.0 - second, first)
        g_ref[here, :] = (straight * keep + crossed * cross).astype(BF16)
        return carry

    lax.fori_loop(0, p_ref.shape[0] // B, step, 0, unroll=4)
    me = me_ref[0]
    x, y, c = me >> 2, (me >> 1) & 1, me & 1
    j = a_cols_ref[...]
    dev = j >> 4
    key = ((dev & 1) * 4 + (((dev >> 2) - x) & 3)) * 2 + (((dev >> 1) - y) & 1)
    column = lax.broadcasted_iota(jnp.int32, j.shape, 1)
    place = jnp.where(column < KL, places(key, NEAR_STEPS), places(key, FAR_STEPS))
    slot = ((dev - c) & 1) * 8 + place
    row_ref[...] = slot * 16 + (j & 15)
    dev_ref[...] = dev


def lift(p_tiles, p_cols, a_cols):
    table = jax.ShapeDtypeStruct(a_cols.shape, jnp.int32)
    return pl.pallas_call(
        lift_kernel,
        out_shape=(jax.ShapeDtypeStruct(p_tiles.shape, BF16), table, table),
        in_specs=[SCALARS, SCALARS, VECTORS, VECTORS],
        out_specs=(VECTORS, VECTORS, VECTORS),
        compiler_params=pltpu.CompilerParams(vmem_limit_bytes=ALL),
    )(lax.axis_index("rows").astype(jnp.int32)[None], p_cols.T, p_tiles, a_cols)


def left_kernel(g_ref, a_ref, w_ref):
    def step(n, carry):
        here = pl.ds(pl.multiple_of(n * 2 * B, 2 * B), 2 * B)
        g_t = g_ref[here, :].T
        a_two = a_ref[here, :]
        for m in (0, 1):
            w_ref[2 * n + m] = jnp.dot(
                g_t[:, m * B : (m + 1) * B],
                a_two[m * B : (m + 1) * B, :],
                preferred_element_type=F32,
            ).astype(BF16)
        return carry

    lax.fori_loop(0, w_ref.shape[0] // 2, step, 0, unroll=2)


def left(lifted, a_tiles):
    rows = a_tiles.shape[0] // B
    width = a_tiles.shape[1]
    return pl.pallas_call(
        left_kernel,
        out_shape=jax.ShapeDtypeStruct((rows, 2 * B, width), BF16),
        in_specs=[VECTORS, VECTORS],
        out_specs=VECTORS,
        cost_estimate=cost(3.0),
        compiler_params=pltpu.CompilerParams(vmem_limit_bytes=LIMIT),
    )(lifted, a_tiles)


def add_products(k_from, k_to, unroll, row_ref, dev_ref, pieces, w_ref, panel, acc, sems):
    copies = []
    start = 0
    for n, piece in enumerate(pieces):
        size = piece.shape[0]
        copies.append(
            pltpu.make_async_copy(piece, panel.at[pl.ds(start, size), :], sems.at[n])
        )
        copies[-1].start()
        start += size
    acc[...] = jnp.zeros_like(acc)
    for copy in copies:
        copy.wait()
    blank = jnp.zeros((B, 2 * B), BF16)

    def step(i, carry):
        for k in range(k_from, k_to, 2):
            upper = panel[pl.ds(pl.multiple_of(row_ref[i, k] * B, B), B), :]
            lower = panel[pl.ds(pl.multiple_of(row_ref[i, k + 1] * B, B), B), :]
            right = jnp.concatenate(
                [
                    jnp.concatenate([upper, blank], axis=1),
                    jnp.concatenate([blank, lower], axis=1),
                ],
                axis=0,
            )
            both = jnp.dot(
                w_ref[i, :, k * B : (k + 2) * B], right, preferred_element_type=F32
            )
            acc[dev_ref[i, k]] += both[:, : 2 * B]
            acc[dev_ref[i, k + 1]] += both[:, 2 * B :]
        return carry

    lax.fori_loop(0, w_ref.shape[0], step, 0, unroll=unroll)


def near_kernel(count, row_ref, dev_ref, *refs):
    w_ref, out_ref, panel, acc, sems = refs[count:]
    add_products(0, KL, 2, row_ref, dev_ref, refs[:count], w_ref, panel, acc, sems)

    def finish(d, carry):
        out_ref[d] = acc[d].astype(BF16)
        return carry

    lax.fori_loop(0, acc.shape[0], finish, 0, unroll=2)


def far_kernel(count, row_ref, dev_ref, *refs):
    w_ref, near_ref, out_ref, panel, acc, sems, mixed = refs[count:]
    ka = row_ref.shape[1]
    add_products(KL, ka, 4, row_ref, dev_ref, refs[:count], w_ref, panel, acc, sems)

    def finish(d, carry):
        lanes = pl.ds(pl.multiple_of(d * 2 * B, 2 * B), 2 * B)
        slot = d % 2
        mixed[slot, pl.ds(0, 2 * B, stride=2), :] = near_ref[d].astype(F32)
        mixed[slot, pl.ds(1, 2 * B, stride=2), :] = acc[d]
        out_ref[:, :, lanes] = mixed[slot].astype(BF16).reshape(2 * B, 2, 2 * B)
        return carry

    lax.fori_loop(0, acc.shape[0], finish, 0, unroll=2)


def products(kernel, row_of, dev_of, pieces, others, out_shape, more, micros):
    rows = sum(piece.shape[0] for piece in pieces)
    devs = rows // (16 * B)
    return pl.pallas_call(
        functools.partial(kernel, len(pieces)),
        out_shape=jax.ShapeDtypeStruct(out_shape, BF16),
        in_specs=[SCALARS] * 2 + [VECTORS] * (len(pieces) + len(others)),
        out_specs=VECTORS,
        scratch_shapes=[
            pltpu.VMEM((rows, 2 * B), BF16),
            pltpu.VMEM((devs, 2 * B, 2 * B), F32),
            pltpu.SemaphoreType.DMA((len(pieces),)),
            *more,
        ],
        cost_estimate=cost(micros),
        compiler_params=pltpu.CompilerParams(vmem_limit_bytes=LIMIT),
    )(row_of, dev_of, *pieces, *others)


def near_half(row_of, dev_of, pieces, w):
    devs = sum(piece.shape[0] for piece in pieces) // (16 * B)
    shape = (devs, 2 * B, 2 * B)
    return products(near_kernel, row_of, dev_of, pieces, (w,), shape, (), 5.0)


def far_half(row_of, dev_of, pieces, w, near):
    shape = (2 * B, 2, near.shape[0] * 2 * B)
    more = (pltpu.VMEM((2, 4 * B, 2 * B), F32),)
    return products(far_kernel, row_of, dev_of, pieces, (w, near), shape, more, 4.0)


def swapped(piece):
    return lax.ppermute(piece, "rows", CORE_SWAP)


def per_device(a_tiles, a_cols, p_tiles, p_cols, band_shift):
    count = lax.axis_size("blk")
    own, row_of, dev_of = lift(p_tiles, p_cols, a_cols)
    near_held = [own]
    for step in NEAR_STEPS[:4]:
        near_held.append(moved(step, near_held))

    def turned(steps):
        pairs = [(s, (s - steps) % count) for s in range(count)]
        return lambda value: lax.ppermute(value, "blk", pairs)

    band = lax.switch(band_shift[0] - 1, [turned(n) for n in range(1, count)], own)
    *near_held, band = lax.optimization_barrier((*near_held, band))
    far_held = [band]
    for step in FAR_STEPS[:3]:
        far_held.append(moved(step, far_held))
    for step in NEAR_STEPS[4:]:
        near_held.append(moved(step, near_held))
    w = left(own, a_tiles)
    *far_held, w = lax.optimization_barrier((*far_held, w))
    near_pieces = near_held + [swapped(piece) for piece in near_held]
    near = near_half(row_of, dev_of, near_pieces, w)
    for step in FAR_STEPS[3:]:
        far_held.append(moved(step, far_held))
    *far_late, near = lax.optimization_barrier((*far_held[4:], near))
    far_held[4:] = far_late
    far_pieces = far_held + [swapped(piece) for piece in far_held]
    return far_half(row_of, dev_of, far_pieces, w, near)


def solution(mesh):
    return jax.shard_map(
        per_device,
        mesh=mesh,
        in_specs=(
            P(("blk", "rows"), None),
            P(("blk", "rows"), None),
            P(("blk", "rows"), None),
            P(("blk", "rows"), None),
            P(),
        ),
        out_specs=P(("blk", "rows"), None, None),
        check_vma=False,
    )
```

```python
import functools

import jax
import jax.numpy as jnp
from jax import lax
from jax.experimental import pallas as pl
from jax.experimental.pallas import tpu as pltpu
from jax.sharding import PartitionSpec as P

B = 64
KL = 12
F32 = jnp.float32
BF16 = jnp.bfloat16
ALL = 60 * 1024 * 1024
LIMIT = 16 * 1024 * 1024
SCALARS = pl.BlockSpec(memory_space=pltpu.SMEM)
VECTORS = pl.BlockSpec(memory_space=pltpu.VMEM)


def cost(micros):
    return pl.CostEstimate(flops=0, bytes_accessed=int(micros * 3.5e6), transcendentals=0)


def rows_id(x, y, c):
    return (x * 2 + y) * 2 + c


def rows_pairs(move):
    return [
        (rows_id(x, y, c), rows_id(*move(x, y, c)))
        for x in range(4)
        for y in range(2)
        for c in range(2)
    ]


X_UP, X_DOWN, Y_OVER, BOTH = (1, 0), (3, 0), (0, 1), (1, 1)
NEAR_STEPS = (
    (0, X_UP, X_UP),
    (0, X_DOWN, X_DOWN),
    (0, Y_OVER, Y_OVER),
    (0, BOTH, BOTH),
    (3, X_DOWN, X_DOWN),
    (1, X_UP, X_UP),
    (4, X_UP, X_UP),
)
FAR_STEPS = (
    (0, X_UP, X_UP),
    (0, X_DOWN, X_DOWN),
    (0, Y_OVER, Y_OVER),
    (1, X_UP, Y_OVER),
    (2, Y_OVER, X_DOWN),
    (3, X_UP, X_DOWN),
    (4, Y_OVER, X_UP),
)
CORE_SWAP = rows_pairs(lambda x, y, c: (x, y, 1 - c))


def moved(step, held):
    source, *moves = step
    pairs = rows_pairs(
        lambda x, y, c: ((x + moves[c][0]) % 4, (y + moves[c][1]) % 2, c)
    )
    return lax.ppermute(held[source], "rows", pairs)


def origins(steps):
    held = [[(0, 0)], [(0, 0)]]
    for source, *moves in steps:
        for c in (0, 1):
            x, y = held[c][source]
            held[c].append(((x - moves[c][0]) % 4, (y - moves[c][1]) % 2))
    return held


def places(key, steps):
    place = jnp.zeros_like(key)
    for core, held in enumerate(origins(steps)):
        for n, (dx, dy) in enumerate(held):
            place = jnp.where(key == (core * 4 + dx) * 2 + dy, n, place)
    return place


def lift_kernel(me_ref, cols_ref, p_ref, a_cols_ref, g_ref, row_ref, dev_ref):
    lane = lax.broadcasted_iota(jnp.int32, (B, 2 * B), 1)
    low = lane < B

    def step(i, carry):
        here = pl.ds(pl.multiple_of(i * B, B), B)
        first = cols_ref[0, i].astype(F32)
        second = cols_ref[1, i].astype(F32)
        straight = p_ref[here, :].astype(F32)
        crossed = pltpu.roll(straight, B, 1)
        keep = jnp.where(low, 1.0 - first, second)
        cross = jnp.where(low, 1.0 - second, first)
        g_ref[here, :] = (straight * keep + crossed * cross).astype(BF16)
        return carry

    lax.fori_loop(0, p_ref.shape[0] // B, step, 0, unroll=4)
    me = me_ref[0]
    x, y, c = me >> 2, (me >> 1) & 1, me & 1
    j = a_cols_ref[...]
    dev = j >> 4
    key = ((dev & 1) * 4 + (((dev >> 2) - x) & 3)) * 2 + (((dev >> 1) - y) & 1)
    column = lax.broadcasted_iota(jnp.int32, j.shape, 1)
    place = jnp.where(column < KL, places(key, NEAR_STEPS), places(key, FAR_STEPS))
    slot = ((dev - c) & 1) * 8 + place
    row_ref[...] = slot * 16 + (j & 15)
    dev_ref[...] = dev


def lift(p_tiles, p_cols, a_cols):
    table = jax.ShapeDtypeStruct(a_cols.shape, jnp.int32)
    return pl.pallas_call(
        lift_kernel,
        out_shape=(jax.ShapeDtypeStruct(p_tiles.shape, BF16), table, table),
        in_specs=[SCALARS, SCALARS, VECTORS, VECTORS],
        out_specs=(VECTORS, VECTORS, VECTORS),
        compiler_params=pltpu.CompilerParams(vmem_limit_bytes=ALL),
    )(lax.axis_index("rows").astype(jnp.int32)[None], p_cols.T, p_tiles, a_cols)


def left_kernel(g_ref, a_ref, w_ref):
    def step(n, carry):
        here = pl.ds(pl.multiple_of(n * 2 * B, 2 * B), 2 * B)
        g_t = g_ref[here, :].T
        a_two = a_ref[here, :]
        for m in (0, 1):
            w_ref[2 * n + m] = jnp.dot(
                g_t[:, m * B : (m + 1) * B],
                a_two[m * B : (m + 1) * B, :],
                preferred_element_type=F32,
            ).astype(BF16)
        return carry

    lax.fori_loop(0, w_ref.shape[0] // 2, step, 0, unroll=2)


def left(lifted, a_tiles):
    rows = a_tiles.shape[0] // B
    width = a_tiles.shape[1]
    return pl.pallas_call(
        left_kernel,
        out_shape=jax.ShapeDtypeStruct((rows, 2 * B, width), BF16),
        in_specs=[VECTORS, VECTORS],
        out_specs=VECTORS,
        cost_estimate=cost(3.0),
        compiler_params=pltpu.CompilerParams(vmem_limit_bytes=LIMIT),
    )(lifted, a_tiles)


def add_products(k_from, k_to, unroll, row_ref, dev_ref, pieces, w_ref, panel, acc, sems):
    copies = []
    start = 0
    for n, piece in enumerate(pieces):
        size = piece.shape[0]
        copies.append(
            pltpu.make_async_copy(piece, panel.at[pl.ds(start, size), :], sems.at[n])
        )
        copies[-1].start()
        start += size
    acc[...] = jnp.zeros_like(acc)
    for copy in copies:
        copy.wait()
    blank = jnp.zeros((B, 2 * B), BF16)

    def step(i, carry):
        for k in range(k_from, k_to, 2):
            upper = panel[pl.ds(pl.multiple_of(row_ref[i, k] * B, B), B), :]
            lower = panel[pl.ds(pl.multiple_of(row_ref[i, k + 1] * B, B), B), :]
            right = jnp.concatenate(
                [
                    jnp.concatenate([upper, blank], axis=1),
                    jnp.concatenate([blank, lower], axis=1),
                ],
                axis=0,
            )
            both = jnp.dot(
                w_ref[i, :, k * B : (k + 2) * B], right, preferred_element_type=F32
            )
            acc[dev_ref[i, k]] += both[:, : 2 * B]
            acc[dev_ref[i, k + 1]] += both[:, 2 * B :]
        return carry

    lax.fori_loop(0, w_ref.shape[0], step, 0, unroll=unroll)


def near_kernel(count, row_ref, dev_ref, *refs):
    w_ref, out_ref, panel, acc, sems = refs[count:]
    add_products(0, KL, 2, row_ref, dev_ref, refs[:count], w_ref, panel, acc, sems)

    def finish(d, carry):
        out_ref[d] = acc[d].astype(BF16)
        return carry

    lax.fori_loop(0, acc.shape[0], finish, 0, unroll=2)


def far_kernel(count, row_ref, dev_ref, *refs):
    w_ref, near_ref, out_ref, panel, acc, sems, mixed = refs[count:]
    ka = row_ref.shape[1]
    add_products(KL, ka, 4, row_ref, dev_ref, refs[:count], w_ref, panel, acc, sems)

    def finish(d, carry):
        lanes = pl.ds(pl.multiple_of(d * 2 * B, 2 * B), 2 * B)
        slot = d % 2
        mixed[slot, pl.ds(0, 2 * B, stride=2), :] = near_ref[d].astype(F32)
        mixed[slot, pl.ds(1, 2 * B, stride=2), :] = acc[d]
        out_ref[:, :, lanes] = mixed[slot].astype(BF16).reshape(2 * B, 2, 2 * B)
        return carry

    lax.fori_loop(0, acc.shape[0], finish, 0, unroll=2)


def products(kernel, row_of, dev_of, pieces, others, out_shape, more, micros):
    rows = sum(piece.shape[0] for piece in pieces)
    devs = rows // (16 * B)
    return pl.pallas_call(
        functools.partial(kernel, len(pieces)),
        out_shape=jax.ShapeDtypeStruct(out_shape, BF16),
        in_specs=[SCALARS] * 2 + [VECTORS] * (len(pieces) + len(others)),
        out_specs=VECTORS,
        scratch_shapes=[
            pltpu.VMEM((rows, 2 * B), BF16),
            pltpu.VMEM((devs, 2 * B, 2 * B), F32),
            pltpu.SemaphoreType.DMA((len(pieces),)),
            *more,
        ],
        cost_estimate=cost(micros),
        compiler_params=pltpu.CompilerParams(vmem_limit_bytes=LIMIT),
    )(row_of, dev_of, *pieces, *others)


def near_half(row_of, dev_of, pieces, w):
    devs = sum(piece.shape[0] for piece in pieces) // (16 * B)
    shape = (devs, 2 * B, 2 * B)
    return products(near_kernel, row_of, dev_of, pieces, (w,), shape, (), 5.0)


def far_half(row_of, dev_of, pieces, w, near):
    shape = (2 * B, 2, near.shape[0] * 2 * B)
    more = (pltpu.VMEM((2, 4 * B, 2 * B), F32),)
    return products(far_kernel, row_of, dev_of, pieces, (w, near), shape, more, 4.0)


def swapped(piece):
    return lax.ppermute(piece, "rows", CORE_SWAP)


def per_device(a_tiles, a_cols, p_tiles, p_cols, band_shift):
    count = lax.axis_size("blk")
    own, row_of, dev_of = lift(p_tiles, p_cols, a_cols)
    near_held = [own]
    for step in NEAR_STEPS[:4]:
        near_held.append(moved(step, near_held))

    def turned(steps):
        pairs = [(s, (s - steps) % count) for s in range(count)]
        return lambda value: lax.ppermute(value, "blk", pairs)

    band = lax.switch(band_shift[0] - 1, [turned(n) for n in range(1, count)], own)
    *near_held, band = lax.optimization_barrier((*near_held, band))
    far_held = [band]
    for step in FAR_STEPS[:3]:
        far_held.append(moved(step, far_held))
    for step in NEAR_STEPS[4:]:
        near_held.append(moved(step, near_held))
    w = left(own, a_tiles)
    *far_held, w = lax.optimization_barrier((*far_held, w))
    near_pieces = near_held + [swapped(piece) for piece in near_held]
    far_others = [swapped(piece) for piece in far_held]
    near_pieces, far_others = lax.optimization_barrier((near_pieces, far_others))
    near = near_half(row_of, dev_of, near_pieces, w)
    for step in FAR_STEPS[3:]:
        far_held.append(moved(step, far_held))
    *far_late, near = lax.optimization_barrier((*far_held[4:], near))
    far_held[4:] = far_late
    far_others += [swapped(piece) for piece in far_late]
    return far_half(row_of, dev_of, far_held + far_others, w, near)


def solution(mesh):
    return jax.shard_map(
        per_device,
        mesh=mesh,
        in_specs=(
            P(("blk", "rows"), None),
            P(("blk", "rows"), None),
            P(("blk", "rows"), None),
            P(("blk", "rows"), None),
            P(),
        ),
        out_specs=P(("blk", "rows"), None, None),
        check_vma=False,
    )
```
